256 devices in a mesh: req: 8 (over x, core), work: 32 (over z, y).
Axes of the slice: x: 4, y: 4, z: 8, core: 2. Of those that a mesh axis runs over, the one named last changes fastest.
Arguments:
- passage_query: bfloat16 [32768, 8192], P('work', 'req'), may hold values from -64 to 64
- passage_key_value: bfloat16 [2, 32768, 1024], P(None, 'work', 'req'), may hold values from -64 to 64
- passage_length: int32 [64], replicated, may hold values from 1 to 4, as said below
- passage_slot: int32 [64], replicated, may hold values from 0 to 63, each once
- cites: int32 [256, 4], P(('req', 'work')), may hold values from 0 to 63, all different within a row
- question_query: bfloat16 [32768, 8192], P(('req', 'work')), may hold values from -64 to 64
- question_key_value: bfloat16 [32768, 2, 1024], P(('req', 'work')), may hold values from -64 to 64
- question_length: int32 [256], P(('req', 'work')), may hold values from 1 to 128, as said below
Outputs:
- passage_output: bfloat16 [32768, 8192], P('work', 'req')
- question_output: bfloat16 [32768, 8192], P(('req', 'work'))
The draws below stay inside these ranges and needn't reach their ends.
Inputs may be any that keep to these rules, and one draw needn't show every extreme that they name: `cites`: each row names 4 different passages and every passage is cited by some request. `passage_length`: some slot holds a passage of 4 blocks. `question_length`: some request has 128 question tokens.
All inputs are finite; a program needn't handle non-finite values.
Results may differ from the reference program's by a relative error of at most 0.0049.
Values may be sent and summed in bfloat16 or wider, within the bound.
No kernel may reach another device: no remote copies, remote signals or barrier semaphores. Data moves between devices by JAX's collectives and lax.ppermute only.
A program may use at most 128 MiB of HBM per device.

```python
import math
import jax
import jax.numpy as jnp
from jax import lax

QUERY_HEADS = 64
KEY_VALUE_HEADS = 8
HEAD_SIZE = 128
BLOCK = 128
PBLK = 4
CITED_PASSAGES = 4
QUESTION_LENGTH = 128
PASSAGE_ROWS = 512
PASSAGE_COUNT = 64
REQUEST_TOTAL = 256


def column_scales(key):
    ranking = jax.random.permutation(key, KEY_VALUE_HEADS).astype(jnp.float32)
    per_group = 0.05 * jnp.exp(math.log(40.0) * ranking / (KEY_VALUE_HEADS - 1))
    return jnp.repeat(per_group, QUERY_HEADS // KEY_VALUE_HEADS * HEAD_SIZE)[None, :]


def draw_passage_query(key, part):
    key = jax.random.fold_in(key, 1)
    return jax.random.normal(key, (PASSAGE_COUNT * PASSAGE_ROWS, QUERY_HEADS * HEAD_SIZE), jnp.float32).astype(jnp.bfloat16)


def draw_passage_key_value(key, part):
    key = jax.random.fold_in(key, 2)
    first_key, second_key = jax.random.split(key)
    key_portion = jax.random.normal(first_key, (PASSAGE_COUNT * PASSAGE_ROWS, KEY_VALUE_HEADS * HEAD_SIZE), jnp.float32)
    value_portion = jax.random.normal(second_key, (PASSAGE_COUNT * PASSAGE_ROWS, KEY_VALUE_HEADS * HEAD_SIZE), jnp.float32)
    return jnp.stack([key_portion, value_portion], axis=0).astype(jnp.bfloat16)


def draw_question_query(key, part):
    key = jax.random.fold_in(key, 3)
    scale_key, main_key = jax.random.split(key)
    column_scale = column_scales(scale_key)
    drawn_rows = jax.random.normal(main_key, (REQUEST_TOTAL * QUESTION_LENGTH, QUERY_HEADS * HEAD_SIZE), jnp.float32)
    return (drawn_rows * column_scale).astype(jnp.bfloat16)


def draw_question_key_value(key, part):
    key = jax.random.fold_in(key, 4)
    first_key, second_key = jax.random.split(key)
    key_portion = jax.random.normal(first_key, (REQUEST_TOTAL * QUESTION_LENGTH, KEY_VALUE_HEADS * HEAD_SIZE), jnp.float32)
    value_portion = jax.random.normal(second_key, (REQUEST_TOTAL * QUESTION_LENGTH, KEY_VALUE_HEADS * HEAD_SIZE), jnp.float32)
    return jnp.stack([key_portion, value_portion], axis=1).astype(jnp.bfloat16)


def draw_passage_length(key, part):
    key = jax.random.fold_in(key, 5)
    first_key, second_key = jax.random.split(key)
    drawn_values = jax.random.randint(first_key, (PASSAGE_COUNT,), 1, PBLK + 1)
    chosen = jax.random.randint(second_key, (), 0, PASSAGE_COUNT)
    return jnp.where(jnp.arange(PASSAGE_COUNT) == chosen, PBLK, drawn_values).astype(jnp.int32)


def draw_question_length(key, part):
    key = jax.random.fold_in(key, 6)
    first_key, second_key = jax.random.split(key)
    drawn_values = jax.random.randint(first_key, (REQUEST_TOTAL,), 1, QUESTION_LENGTH + 1)
    chosen = jax.random.randint(second_key, (), 0, REQUEST_TOTAL)
    return jnp.where(jnp.arange(REQUEST_TOTAL) == chosen, QUESTION_LENGTH, drawn_values).astype(jnp.int32)


def distinct(own_key, rows, count, top, lift):
    order = jax.random.permutation(jax.random.fold_in(own_key, 1), count)
    favour = order
    for power in range(3):
        favour = favour * favour // count
    favour = favour * lift // count
    chance = jax.random.randint(jax.random.fold_in(own_key, 2), (rows, count), 0, 4096) + favour
    fixed_rows = jax.random.permutation(jax.random.fold_in(own_key, 3), rows)[jnp.arange(count) % rows]
    chance = jnp.where(jnp.arange(rows)[:, None] == fixed_rows[None, :], 1 << 14, chance)
    merit = chance * count + jnp.arange(count)
    return lax.top_k(merit.astype(jnp.int32), top)[1].astype(jnp.int32)


def setup_inputs(seed: int = 0) -> dict:
    arg_keys = jax.random.split(jax.random.key(seed), 9)
    return {
        "passage_query": draw_passage_query(jax.random.fold_in(arg_keys[8], 71), 0),
        "passage_key_value": draw_passage_key_value(jax.random.fold_in(arg_keys[8], 71), 0),
        "passage_length": draw_passage_length(jax.random.fold_in(arg_keys[8], 71), 0),
        "passage_slot": jax.random.permutation(arg_keys[3], PASSAGE_COUNT).astype(jnp.int32),
        "cites": distinct(arg_keys[4], REQUEST_TOTAL, PASSAGE_COUNT, CITED_PASSAGES, 1024),
        "question_query": draw_question_query(jax.random.fold_in(arg_keys[8], 71), 0),
        "question_key_value": draw_question_key_value(jax.random.fold_in(arg_keys[8], 71), 0),
        "question_length": draw_question_length(jax.random.fold_in(arg_keys[8], 71), 0),
    }


def single_head_attention(query_matrix, key_matrix, value_matrix, visible_mask):
    scores = jnp.einsum('qgd,pd->gqp', query_matrix, key_matrix, precision=lax.Precision.HIGHEST) * (1.0 / math.sqrt(HEAD_SIZE))
    scores = jnp.where(visible_mask[None], scores, -jnp.inf)
    highest = lax.optimization_barrier(jnp.max(scores, axis=-1, keepdims=True))
    raised = jnp.exp(scores - highest)
    weights = (raised / lax.optimization_barrier(jnp.sum(raised, axis=-1, keepdims=True))).astype(jnp.bfloat16)
    weights = lax.optimization_barrier(weights).astype(jnp.float32)
    return jnp.einsum('gqp,pd->qgd', weights, value_matrix, precision=lax.Precision.HIGHEST)

def every_head_output(query_matrix, key_matrix, value_matrix, visible_mask):
    collected_outputs = [single_head_attention(query_matrix[:, current_head], key_matrix[:, current_head], value_matrix[:, current_head], visible_mask) for current_head in range(KEY_VALUE_HEADS)]
    return jnp.stack(collected_outputs, axis=1)

def passage_attention_block(packed):
    query_matrix, key_matrix, value_matrix, blocks = packed
    query_group_size = QUERY_HEADS // KEY_VALUE_HEADS
    position = jnp.arange(PASSAGE_ROWS)
    visible_mask = position[None, :] <= position[:, None]
    head_output = every_head_output(query_matrix.astype(jnp.float32).reshape(PASSAGE_ROWS, KEY_VALUE_HEADS, query_group_size, HEAD_SIZE), key_matrix.astype(jnp.float32).reshape(PASSAGE_ROWS, KEY_VALUE_HEADS, HEAD_SIZE), value_matrix.astype(jnp.float32).reshape(PASSAGE_ROWS, KEY_VALUE_HEADS, HEAD_SIZE), visible_mask)
    living = position < blocks * BLOCK
    return jnp.where(living[:, None], head_output.reshape(PASSAGE_ROWS, QUERY_HEADS * HEAD_SIZE), 0.0).astype(jnp.bfloat16)

def reference(passage_query, passage_key_value, passage_length, passage_slot, cites, question_query, question_key_value, question_length):
    passage_output = lax.map(passage_attention_block, (passage_query.reshape(PASSAGE_COUNT, PASSAGE_ROWS, QUERY_HEADS * HEAD_SIZE), passage_key_value[0].reshape(PASSAGE_COUNT, PASSAGE_ROWS, KEY_VALUE_HEADS * HEAD_SIZE), passage_key_value[1].reshape(PASSAGE_COUNT, PASSAGE_ROWS, KEY_VALUE_HEADS * HEAD_SIZE), passage_length))
    passage_output = passage_output.reshape(PASSAGE_COUNT * PASSAGE_ROWS, QUERY_HEADS * HEAD_SIZE)
    slot_numbers = passage_slot[cites]
    referenced_blocks = passage_length[slot_numbers]
    saved_values = passage_key_value.reshape(2, PASSAGE_COUNT, PASSAGE_ROWS, KEY_VALUE_HEADS * HEAD_SIZE)
    query_group_size = QUERY_HEADS // KEY_VALUE_HEADS

    def question_attention_block(packed):
        query_matrix, passage_own_rows, chosen, blocks, length = packed
        referenced_rows = jnp.take(saved_values, chosen, axis=1)
        key_matrix = jnp.concatenate([referenced_rows[0].reshape(CITED_PASSAGES * PASSAGE_ROWS, KEY_VALUE_HEADS * HEAD_SIZE), passage_own_rows[:, 0]], axis=0)
        value_matrix = jnp.concatenate([referenced_rows[1].reshape(CITED_PASSAGES * PASSAGE_ROWS, KEY_VALUE_HEADS * HEAD_SIZE), passage_own_rows[:, 1]], axis=0)
        inner = jnp.arange(CITED_PASSAGES * PASSAGE_ROWS) % PASSAGE_ROWS
        owner = jnp.arange(CITED_PASSAGES * PASSAGE_ROWS) // PASSAGE_ROWS
        row_blocks = lax.optimization_barrier(jnp.sum(jnp.where(owner[:, None] == jnp.arange(CITED_PASSAGES)[None, :], blocks[None, :], 0), axis=1))
        passage_ok = inner < row_blocks * BLOCK
        position = jnp.arange(QUESTION_LENGTH)
        own_ok = position[None, :] <= position[:, None]
        visible_mask = jnp.concatenate([jnp.broadcast_to(passage_ok[None, :], (QUESTION_LENGTH, CITED_PASSAGES * PASSAGE_ROWS)), own_ok], axis=1)
        head_output = every_head_output(query_matrix.astype(jnp.float32).reshape(QUESTION_LENGTH, KEY_VALUE_HEADS, query_group_size, HEAD_SIZE), key_matrix.astype(jnp.float32).reshape(-1, KEY_VALUE_HEADS, HEAD_SIZE), value_matrix.astype(jnp.float32).reshape(-1, KEY_VALUE_HEADS, HEAD_SIZE), visible_mask)
        living = position < length
        return jnp.where(living[:, None], head_output.reshape(QUESTION_LENGTH, QUERY_HEADS * HEAD_SIZE), 0.0).astype(jnp.bfloat16)
    question_output = lax.map(question_attention_block, (question_query.reshape(REQUEST_TOTAL, QUESTION_LENGTH, QUERY_HEADS * HEAD_SIZE), question_key_value.reshape(REQUEST_TOTAL, QUESTION_LENGTH, 2, KEY_VALUE_HEADS * HEAD_SIZE), slot_numbers, referenced_blocks, question_length))
    return (passage_output, question_output.reshape(REQUEST_TOTAL * QUESTION_LENGTH, QUERY_HEADS * HEAD_SIZE))
```

```python
import math

import jax
import jax.numpy as jnp
from jax import lax
from jax.experimental import pallas as pl
from jax.experimental.pallas import tpu as pltpu
from jax.sharding import PartitionSpec as P

QUERY_HEADS = 64
KEY_VALUE_HEADS = 8
GROUP = QUERY_HEADS // KEY_VALUE_HEADS
HEAD_SIZE = 128
BLOCK = 128
PBLK = 4
CITED_PASSAGES = 4
QUESTION_LENGTH = 128
PASSAGE_ROWS = 512
SCALE = math.log2(math.e) / math.sqrt(HEAD_SIZE)
LOW = -1e30
TILE = 32
MOST = CITED_PASSAGES * PBLK
DOT_NT = (((1,), (1,)), ((), ()))


def stack_heads(ref_rows):
    return jnp.concatenate(
        [ref_rows[:, h * HEAD_SIZE : (h + 1) * HEAD_SIZE] for h in range(GROUP)], axis=0
    )


def with_ones(values):
    return jnp.concatenate([values, jnp.ones_like(values)], axis=1)


def passage_kernel(blocks_ref, q_ref, kv_ref, out_ref):
    slot = pl.program_id(0)
    blocks = blocks_ref[slot]
    rows = GROUP * BLOCK
    row = lax.broadcasted_iota(jnp.int32, (rows, BLOCK), 0) % BLOCK
    column = lax.broadcasted_iota(jnp.int32, (rows, BLOCK), 1)
    causal = column <= row
    for i in range(PBLK):
        place = slice(i * BLOCK, (i + 1) * BLOCK)

        @pl.when(i < blocks)
        def _():
            q = stack_heads(q_ref[place, :])
            k = kv_ref[0, : (i + 1) * BLOCK, :]
            v = with_ones(kv_ref[1, : (i + 1) * BLOCK, :])
            s = lax.dot_general(q, k, DOT_NT, preferred_element_type=jnp.float32)
            last = jnp.where(causal, s[:, i * BLOCK :], LOW)
            s = last if i == 0 else jnp.concatenate([s[:, : i * BLOCK], last], axis=1)
            m = jnp.max(s, axis=1, keepdims=True)
            p = jnp.exp2((s - m) * SCALE).astype(jnp.bfloat16)
            o = jnp.dot(p, v, preferred_element_type=jnp.float32)
            o = (o[:, :HEAD_SIZE] / o[:, HEAD_SIZE:]).astype(jnp.bfloat16)
            for h in range(GROUP):
                out_ref[place, h * HEAD_SIZE : (h + 1) * HEAD_SIZE] = o[h * BLOCK : (h + 1) * BLOCK]

        @pl.when(i >= blocks)
        def _():
            out_ref[place, :] = jnp.zeros((BLOCK, GROUP * HEAD_SIZE), jnp.bfloat16)


def passage_attention(blocks, query, key_value):
    slots = query.shape[0] // PASSAGE_ROWS
    width = GROUP * HEAD_SIZE
    return pl.pallas_call(
        passage_kernel,
        out_shape=jax.ShapeDtypeStruct(query.shape, jnp.bfloat16),
        grid_spec=pltpu.PrefetchScalarGridSpec(
            num_scalar_prefetch=1,
            grid=(slots,),
            in_specs=[
                pl.BlockSpec((PASSAGE_ROWS, width), lambda s, b: (s, 0)),
                pl.BlockSpec((2, PASSAGE_ROWS, HEAD_SIZE), lambda s, b: (0, s, 0)),
            ],
            out_specs=pl.BlockSpec((PASSAGE_ROWS, width), lambda s, b: (s, 0)),
        ),
        compiler_params=pltpu.CompilerParams(vmem_limit_bytes=40 * 1024 * 1024),
        cost_estimate=pl.CostEstimate(
            flops=slots * 4 * 1024 * 512 * 512, bytes_accessed=5 * 1024 * 1024, transcendentals=0
        ),
    )(blocks, query, key_value)


def question_kernel(table_ref, count_ref, length_ref, q_ref, own_ref, kv_ref, out_ref, store, sems):
    request = pl.program_id(0)

    @pl.when(request == 0)
    def _():
        copies = [
            pltpu.make_async_copy(kv_ref.at[part], store.at[part], sems.at[part]) for part in range(2)
        ]
        for copy in copies:
            copy.start()
        for copy in copies:
            copy.wait()

    length = length_ref[request]
    count = count_ref[request]
    out_ref[...] = jnp.zeros_like(out_ref)
    rows = GROUP * TILE
    row = lax.broadcasted_iota(jnp.int32, (rows, BLOCK), 0) % TILE
    column = lax.broadcasted_iota(jnp.int32, (rows, BLOCK), 1)

    def attend(cited):
        places = [table_ref[request * (MOST + 1) + i] for i in range(cited)]
        extra = jnp.where(count < cited, LOW, 0.0)

        def tile_step(tile, carry):
            first = pl.multiple_of(tile * TILE, TILE)
            q = stack_heads(q_ref[0, pl.ds(first, TILE), :])
            k = jnp.concatenate([own_ref[0, 0]] + [store[0, at] for at in places], axis=0)
            v = jnp.concatenate([own_ref[0, 1]] + [store[1, at] for at in places], axis=0)
            s = lax.dot_general(q, k, DOT_NT, preferred_element_type=jnp.float32)
            s = jnp.concatenate(
                [
                    jnp.where(column <= row + first, s[:, :BLOCK], LOW),
                    s[:, BLOCK:-BLOCK],
                    s[:, -BLOCK:] + extra,
                ],
                axis=1,
            )
            m = jnp.max(s, axis=1, keepdims=True)
            p = jnp.exp2((s - m) * SCALE).astype(jnp.bfloat16)
            o = jnp.dot(p, with_ones(v), preferred_element_type=jnp.float32)
            o = o[:, :HEAD_SIZE] / o[:, HEAD_SIZE:]
            o = jnp.where(row + first < length, o, 0.0).astype(jnp.bfloat16)
            for h in range(GROUP):
                out_ref[0, pl.ds(first, TILE), h * HEAD_SIZE : (h + 1) * HEAD_SIZE] = o[
                    h * TILE : (h + 1) * TILE
                ]
            return carry

        lax.fori_loop(0, (length + TILE - 1) // TILE, tile_step, 0)

    for cited in range(CITED_PASSAGES + 1, MOST + 2, 2):
        pl.when((count + 1) // 2 * 2 + 1 - (count % 2) * 2 == cited)(lambda cited=cited: attend(cited))


def question_attention(table, count, length, query, own, key_value):
    requests, rows, width = query.shape
    return pl.pallas_call(
        question_kernel,
        out_shape=jax.ShapeDtypeStruct(query.shape, jnp.bfloat16),
        grid_spec=pltpu.PrefetchScalarGridSpec(
            num_scalar_prefetch=3,
            grid=(requests,),
            in_specs=[
                pl.BlockSpec((1, rows, width), lambda r, *_: (r, 0, 0)),
                pl.BlockSpec((1, 2, rows, HEAD_SIZE), lambda r, *_: (r, 0, 0, 0)),
                pl.BlockSpec(memory_space=pl.ANY),
            ],
            out_specs=pl.BlockSpec((1, rows, width), lambda r, *_: (r, 0, 0)),
            scratch_shapes=[
                pltpu.VMEM(key_value.shape, jnp.bfloat16),
                pltpu.SemaphoreType.DMA((2,)),
            ],
        ),
        compiler_params=pltpu.CompilerParams(vmem_limit_bytes=48 * 1024 * 1024),
        cost_estimate=pl.CostEstimate(
            flops=4 * 1024 * 1024 * 1024, bytes_accessed=24 * 1024 * 1024, transcendentals=0
        ),
    )(table, count, length, query, own, key_value)


def slot_lookup(cited_ids, lookup_table):
    matches = cited_ids[..., None] == jnp.arange(lookup_table.shape[0])
    return jnp.sum(jnp.where(matches, lookup_table, 0), axis=-1)


def block_table(slots, blocks):
    ends = jnp.cumsum(blocks, axis=1)
    begins = ends - blocks
    index = jnp.arange(MOST + 1)[None, None, :]
    inside = (index >= begins[..., None]) & (index < ends[..., None])
    number = slots[..., None] * PBLK + index - begins[..., None]
    return jnp.sum(jnp.where(inside, number, 0), axis=1), ends[:, -1]


def body(
    passage_query,
    passage_key_value,
    passage_length,
    passage_slot,
    cites,
    question_query,
    question_key_value,
    question_length,
):
    all_rows = lax.all_gather(passage_key_value, "work", axis=1, tiled=True)
    all_blocks = all_rows.reshape(2, -1, BLOCK, HEAD_SIZE)

    width = GROUP * HEAD_SIZE
    query = question_query.reshape(QUESTION_LENGTH, KEY_VALUE_HEADS, width)
    own = question_key_value.reshape(QUESTION_LENGTH, 2, KEY_VALUE_HEADS, HEAD_SIZE)
    query = lax.all_to_all(jnp.transpose(query, (1, 0, 2)), "req", 0, 0, tiled=True)
    own = lax.all_to_all(jnp.transpose(own, (2, 1, 0, 3)), "req", 0, 0, tiled=True)

    facts = jnp.concatenate([cites, question_length[:, None]], axis=1)
    facts = lax.all_gather(facts, "req", axis=0, tiled=True)
    slots = slot_lookup(facts[:, :CITED_PASSAGES], passage_slot)
    table, count = block_table(slots, slot_lookup(slots, passage_length))

    slot_total = passage_query.shape[0] // PASSAGE_ROWS
    my_blocks = lax.dynamic_slice_in_dim(
        passage_length, lax.axis_index("work") * slot_total, slot_total
    )
    passage_output = passage_attention(my_blocks, passage_query, passage_key_value)

    answer = question_attention(
        table.reshape(-1), count, facts[:, CITED_PASSAGES], query, own, all_blocks
    )
    answer = lax.all_to_all(answer, "req", 0, 0, tiled=True)
    question_output = jnp.transpose(answer, (1, 0, 2)).reshape(QUESTION_LENGTH, -1)
    return (passage_output, question_output)


def solution(mesh):
    return jax.shard_map(
        body,
        mesh=mesh,
        in_specs=(
            P("work", "req"),
            P(None, "work", "req"),
            P(),
            P(),
            P(("req", "work"), None),
            P(("req", "work"), None),
            P(("req", "work"), None, None),
            P(("req", "work")),
        ),
        out_specs=(P("work", "req"), P(("req", "work"), None)),
        check_vma=False,
    )
```

```python
import math

import jax
import jax.numpy as jnp
from jax import lax
from jax.experimental import pallas as pl
from jax.experimental.pallas import tpu as pltpu
from jax.sharding import PartitionSpec as P

QUERY_HEADS = 64
KEY_VALUE_HEADS = 8
GROUP = QUERY_HEADS // KEY_VALUE_HEADS
HEAD_SIZE = 128
BLOCK = 128
PBLK = 4
CITED_PASSAGES = 4
QUESTION_LENGTH = 128
PASSAGE_ROWS = 512
SCALE = math.log2(math.e) / math.sqrt(HEAD_SIZE)
LOW = -1e30
TILE = 64
LOTS = 2
MOST = CITED_PASSAGES * PBLK
WORK_Z, WORK_Y = 8, 4
SLOTS = 2
KEPT = 6
EXTRA = SLOTS * PBLK - KEPT
FIRST = 6
SECOND = WORK_Z * EXTRA - FIRST
GATHERED = WORK_Z * WORK_Y * KEPT
Z_ORDER = (0, 1, 3, 5, 7, 6, 4, 2)
Y_ORDER = (0, 1, 3, 2)
OWN_ROW = GROUP * QUESTION_LENGTH
FACT_ROW = OWN_ROW + 2 * QUESTION_LENGTH
PAYLOAD = FACT_ROW + 16
DOT_NT = (((1,), (1,)), ((), ()))


def stack_heads(ref_rows):
    return jnp.concatenate(
        [ref_rows[:, h * HEAD_SIZE : (h + 1) * HEAD_SIZE] for h in range(GROUP)], axis=0
    )


def with_ones(values):
    return jnp.concatenate([values, jnp.ones_like(values)], axis=1)


def passage_kernel(blocks_ref, q_ref, kv_ref, out_ref):
    slot = pl.program_id(0)
    blocks = blocks_ref[slot]
    rows = GROUP * BLOCK
    row = lax.broadcasted_iota(jnp.int32, (rows, BLOCK), 0) % BLOCK
    column = lax.broadcasted_iota(jnp.int32, (rows, BLOCK), 1)
    causal = column <= row
    for i in range(PBLK):
        place = slice(i * BLOCK, (i + 1) * BLOCK)

        @pl.when(i < blocks)
        def _():
            q = stack_heads(q_ref[place, :])
            k = kv_ref[0, : (i + 1) * BLOCK, :]
            v = with_ones(kv_ref[1, : (i + 1) * BLOCK, :])
            s = lax.dot_general(q, k, DOT_NT, preferred_element_type=jnp.float32)
            last = jnp.where(causal, s[:, i * BLOCK :], LOW)
            s = last if i == 0 else jnp.concatenate([s[:, : i * BLOCK], last], axis=1)
            m = jnp.max(s, axis=1, keepdims=True)
            p = jnp.exp2((s - m) * SCALE).astype(jnp.bfloat16)
            o = jnp.dot(p, v, preferred_element_type=jnp.float32)
            o = (o[:, :HEAD_SIZE] / o[:, HEAD_SIZE:]).astype(jnp.bfloat16)
            for h in range(GROUP):
                out_ref[place, h * HEAD_SIZE : (h + 1) * HEAD_SIZE] = o[h * BLOCK : (h + 1) * BLOCK]

        @pl.when(i >= blocks)
        def _():
            out_ref[place, :] = jnp.zeros((BLOCK, GROUP * HEAD_SIZE), jnp.bfloat16)


def passage_attention(blocks, query, key_value):
    slots = query.shape[0] // PASSAGE_ROWS
    width = GROUP * HEAD_SIZE
    return pl.pallas_call(
        passage_kernel,
        out_shape=jax.ShapeDtypeStruct(query.shape, jnp.bfloat16),
        grid_spec=pltpu.PrefetchScalarGridSpec(
            num_scalar_prefetch=1,
            grid=(slots,),
            in_specs=[
                pl.BlockSpec((PASSAGE_ROWS, width), lambda s, b: (s, 0)),
                pl.BlockSpec((2, PASSAGE_ROWS, HEAD_SIZE), lambda s, b: (0, s, 0)),
            ],
            out_specs=pl.BlockSpec((PASSAGE_ROWS, width), lambda s, b: (s, 0)),
        ),
        compiler_params=pltpu.CompilerParams(vmem_limit_bytes=40 * 1024 * 1024),
        cost_estimate=pl.CostEstimate(
            flops=slots * 4 * 1024 * 512 * 512, bytes_accessed=5 * 1024 * 1024, transcendentals=0
        ),
    )(blocks, query, key_value)


def bundle_kernel(q_ref, k_ref, v_ref, facts_ref, out_ref):
    for h in range(GROUP):
        out_ref[0, h * QUESTION_LENGTH : (h + 1) * QUESTION_LENGTH, :] = q_ref[
            :, h * HEAD_SIZE : (h + 1) * HEAD_SIZE
        ]
    out_ref[0, OWN_ROW : OWN_ROW + QUESTION_LENGTH, :] = k_ref[...].T
    out_ref[0, OWN_ROW + QUESTION_LENGTH : FACT_ROW, :] = v_ref[...]
    out_ref[0, FACT_ROW:, :] = facts_ref[...]


def bundle(query, own, facts):
    width = GROUP * HEAD_SIZE
    return pl.pallas_call(
        bundle_kernel,
        out_shape=jax.ShapeDtypeStruct((KEY_VALUE_HEADS, PAYLOAD, HEAD_SIZE), jnp.bfloat16),
        grid=(KEY_VALUE_HEADS,),
        in_specs=[
            pl.BlockSpec((QUESTION_LENGTH, width), lambda g: (0, g)),
            pl.BlockSpec((QUESTION_LENGTH, HEAD_SIZE), lambda g: (0, g)),
            pl.BlockSpec((QUESTION_LENGTH, HEAD_SIZE), lambda g: (0, KEY_VALUE_HEADS + g)),
            pl.BlockSpec((16, HEAD_SIZE), lambda g: (0, 0)),
        ],
        out_specs=pl.BlockSpec((1, PAYLOAD, HEAD_SIZE), lambda g: (g, 0, 0)),
        cost_estimate=pl.CostEstimate(flops=0, bytes_accessed=5 * 1024 * 1024, transcendentals=0),
    )(query, own, own, facts)


def spread_kernel(in_ref, out_ref):
    for g in range(in_ref.shape[0]):
        for h in range(GROUP):
            first = (g * GROUP + h) * HEAD_SIZE
            out_ref[:, first : first + HEAD_SIZE] = in_ref[
                g, h * QUESTION_LENGTH : (h + 1) * QUESTION_LENGTH, :
            ]


def spread(answer):
    groups = 2
    width = groups * GROUP * HEAD_SIZE
    return pl.pallas_call(
        spread_kernel,
        out_shape=jax.ShapeDtypeStruct((QUESTION_LENGTH, QUERY_HEADS * HEAD_SIZE), jnp.bfloat16),
        grid=(KEY_VALUE_HEADS // groups,),
        in_specs=[pl.BlockSpec((groups, OWN_ROW, HEAD_SIZE), lambda g: (g, 0, 0))],
        out_specs=pl.BlockSpec((QUESTION_LENGTH, width), lambda g: (0, g)),
        cost_estimate=pl.CostEstimate(flops=0, bytes_accessed=4 * 1024 * 1024, transcendentals=0),
    )(answer)


def order_kernel(length_ref, kv_ref, kept_ref, *refs):
    worker = lax.axis_index("work")
    before = 0
    for slot in range(SLOTS):
        length = length_ref[worker * SLOTS + slot]
        for block in range(PBLK):
            rows = slice((slot * PBLK + block) * BLOCK, (slot * PBLK + block + 1) * BLOCK)

            def put(ref, place):
                ref[place, 0] = kv_ref[0, rows, :].T
                ref[place, 1] = kv_ref[1, rows, :]

            place = before + block
            pl.when((block < length) & (place < KEPT))(lambda place=place: put(kept_ref, place))
            if refs:
                pl.when((block < length) & (place >= KEPT))(
                    lambda place=place: put(refs[0], place - KEPT)
                )
        before = before + length


def order(passage_length, key_value):
    shapes = [
        jax.ShapeDtypeStruct((size, 2, BLOCK, HEAD_SIZE), jnp.bfloat16)
        for size in (KEPT, EXTRA)
        if size
    ]
    return pl.pallas_call(
        order_kernel,
        out_shape=shapes,
        in_specs=[pl.BlockSpec(memory_space=pltpu.SMEM), pl.BlockSpec(memory_space=pltpu.VMEM)],
        out_specs=[pl.BlockSpec(memory_space=pltpu.VMEM)] * len(shapes),
        cost_estimate=pl.CostEstimate(flops=0, bytes_accessed=1024 * 1024, transcendentals=0),
    )(passage_length, key_value)


def pack_kernel(place_ref, *refs):
    sources, outs = refs[:-2], refs[-2:]
    blocks = [(source, i) for source in sources for i in range(source.shape[0])]
    for index, (source, i) in enumerate(blocks):
        place = place_ref[index]

        @pl.when((place >= 0) & (place < FIRST))
        def _():
            outs[0][place] = source[i]

        @pl.when(place >= FIRST)
        def _():
            outs[1][place - FIRST] = source[i]


def pack(place, sources):
    return pl.pallas_call(
        pack_kernel,
        out_shape=[
            jax.ShapeDtypeStruct((size, *sources[0].shape[1:]), jnp.bfloat16)
            for size in (FIRST, SECOND)
        ],
        in_specs=[pl.BlockSpec(memory_space=pltpu.SMEM)]
        + [pl.BlockSpec(memory_space=pltpu.VMEM)] * len(sources),
        out_specs=[pl.BlockSpec(memory_space=pltpu.VMEM)] * 2,
        cost_estimate=pl.CostEstimate(flops=0, bytes_accessed=2 * 1024 * 1024, transcendentals=0),
    )(place, *sources)


def question_kernel(table_ref, count_ref, length_ref, in_ref, *refs):
    pieces, out_ref, store, sems = refs[:-3], refs[-3], refs[-2], refs[-1]
    request = pl.program_id(0)
    total = pl.num_programs(0)

    def start(which, carry):
        def one(index, carry):
            place = table_ref[which * (MOST + 1) + index]
            low = 0
            for piece in pieces:
                size = piece.shape[0]

                @pl.when((place >= low) & (place < low + size))
                def _():
                    pltpu.make_async_copy(
                        piece.at[place - low], store.at[which, index], sems.at[which, index]
                    ).start()

                low += size
            return carry

        return lax.fori_loop(0, count_ref[which], one, carry)

    @pl.when(request == 0)
    def _():
        lax.fori_loop(0, total, start, 0)

    length = length_ref[request]
    count = count_ref[request]

    def wait(index, carry):
        pltpu.make_async_copy(
            pieces[0].at[0], store.at[request, index], sems.at[request, index]
        ).wait()
        return carry

    lax.fori_loop(0, count, wait, 0)
    rows = GROUP // LOTS * TILE
    row = lax.broadcasted_iota(jnp.int32, (rows, BLOCK), 0) % TILE
    column = lax.broadcasted_iota(jnp.int32, (rows, BLOCK), 1)

    def attend(cited):
        @pl.when(count < cited)
        def _():
            store[request, cited - 1] = jnp.zeros(store.shape[2:], store.dtype)

        extra = jnp.where(count < cited, LOW, 0.0)

        def tile_step(tile, carry):
            first = pl.multiple_of(tile * TILE, TILE)
            k = [in_ref[0, OWN_ROW : OWN_ROW + BLOCK, :]] + [store[request, i, 0] for i in range(cited)]
            v = [in_ref[0, OWN_ROW + BLOCK : FACT_ROW, :]] + [store[request, i, 1] for i in range(cited)]
            k = jnp.concatenate(k, axis=1)
            v = with_ones(jnp.concatenate(v, axis=0))
            lot = GROUP // LOTS

            def score(heads):
                q = jnp.concatenate(
                    [in_ref[0, pl.ds(h * QUESTION_LENGTH + first, TILE), :] for h in heads], axis=0
                )
                s = jnp.dot(q, k, preferred_element_type=jnp.float32)
                return jnp.concatenate(
                    [
                        jnp.where(column <= row + first, s[:, :BLOCK], LOW),
                        s[:, BLOCK:-BLOCK],
                        s[:, -BLOCK:] + extra,
                    ],
                    axis=1,
                )

            def finish(heads, s):
                m = jnp.max(s, axis=1, keepdims=True)
                p = jnp.exp2((s - m) * SCALE).astype(jnp.bfloat16)
                o = jnp.dot(p, v, preferred_element_type=jnp.float32)
                o = o[:, :HEAD_SIZE] / o[:, HEAD_SIZE:]
                o = jnp.where(row + first < length, o, 0.0).astype(jnp.bfloat16)
                for i, h in enumerate(heads):
                    out_ref[0, pl.ds(h * QUESTION_LENGTH + first, TILE), :] = o[
                        i * TILE : (i + 1) * TILE
                    ]

            lots = [range(i * lot, (i + 1) * lot) for i in range(LOTS)]
            s = score(lots[0])
            for i in range(LOTS):
                following = score(lots[i + 1]) if i + 1 < LOTS else None
                finish(lots[i], s)
                s = following
            return carry

        lax.fori_loop(0, (length + TILE - 1) // TILE, tile_step, 0)

    def clear(tile, carry):
        for h in range(GROUP):
            out_ref[0, pl.ds(h * QUESTION_LENGTH + pl.multiple_of(tile * TILE, TILE), TILE), :] = (
                jnp.zeros((TILE, HEAD_SIZE), out_ref.dtype)
            )
        return carry

    lax.fori_loop((length + TILE - 1) // TILE, QUESTION_LENGTH // TILE, clear, 0)

    for cited in range(CITED_PASSAGES + 1, MOST + 2, 2):
        pl.when(count // 2 * 2 + 1 == cited)(lambda cited=cited: attend(cited))


def question_attention(table, count, length, payload, pieces):
    requests = payload.shape[0]
    return pl.pallas_call(
        question_kernel,
        out_shape=jax.ShapeDtypeStruct((requests, OWN_ROW, HEAD_SIZE), jnp.bfloat16),
        grid_spec=pltpu.PrefetchScalarGridSpec(
            num_scalar_prefetch=3,
            grid=(requests,),
            in_specs=[pl.BlockSpec((1, PAYLOAD, HEAD_SIZE), lambda r, *_: (r, 0, 0))]
            + [pl.BlockSpec(memory_space=pl.ANY)] * len(pieces),
            out_specs=pl.BlockSpec((1, OWN_ROW, HEAD_SIZE), lambda r, *_: (r, 0, 0)),
            scratch_shapes=[
                pltpu.VMEM((requests, MOST + 1, *pieces[0].shape[1:]), jnp.bfloat16),
                pltpu.SemaphoreType.DMA((requests, MOST)),
            ],
        ),
        compiler_params=pltpu.CompilerParams(vmem_limit_bytes=40 * 1024 * 1024),
        cost_estimate=pl.CostEstimate(
            flops=4 * 1024 * 1024 * 1024, bytes_accessed=24 * 1024 * 1024, transcendentals=0
        ),
    )(table, count, length, payload, *pieces)


def step_z(array, by):
    steps = [
        (z * WORK_Y + y, (z + by) % WORK_Z * WORK_Y + y) for z in range(WORK_Z) for y in range(WORK_Y)
    ]
    return lax.ppermute(array, "work", steps)


def step_y(array, by):
    steps = [
        (z * WORK_Y + y, z * WORK_Y + (y + by) % WORK_Y) for z in range(WORK_Z) for y in range(WORK_Y)
    ]
    return lax.ppermute(array, "work", steps)


def ring_z(chunk):
    out = [chunk]
    up = down = chunk
    for _ in range(WORK_Z // 2 - 1):
        up, down = step_z(up, 1), step_z(down, -1)
        out += [up, down]
    half = chunk.shape[0] // 2
    return out + [step_z(up[:half], 1), step_z(down[half:], -1)]


def ring_y(chunk):
    half = chunk.shape[0] // 2
    up, down = step_y(chunk, 1), step_y(chunk, -1)
    return [chunk, up, down, step_y(up[:half], 1), step_y(down[half:], -1)]


def pick(index, values):
    values = jnp.asarray(values, jnp.int32)
    return jnp.sum(
        jnp.where(index[..., None] == jnp.arange(values.shape[0]), values, 0), axis=-1
    )


def block_places(passage_length, y):
    lengths = passage_length.reshape(WORK_Z, WORK_Y, SLOTS)
    ahead = jnp.concatenate([jnp.zeros_like(lengths[..., :1]), lengths[..., :1]], axis=-1)
    at = ahead[..., None] + jnp.arange(PBLK)
    worker = jnp.arange(WORK_Z)[:, None] * WORK_Y + jnp.arange(WORK_Y)
    gathered = worker[..., None, None] * KEPT + at
    if not EXTRA:
        return gathered.reshape(-1, PBLK), None, None
    beyond = jnp.maximum(jnp.sum(lengths, axis=-1) - KEPT, 0)
    earlier = jnp.arange(WORK_Z)
    earlier = (earlier[:, None] < earlier[None, :]).astype(jnp.int32)
    begins = jnp.sum(earlier[:, :, None] * beyond[:, None, :], axis=0)
    index = jnp.arange(EXTRA)
    lists = jnp.where(index < beyond[..., None], begins[..., None] + index, -1)
    place = begins[..., None, None] + at - KEPT
    y_place = pick((y - jnp.arange(WORK_Y)) % WORK_Y, Y_ORDER)[None, :, None, None]
    place = jnp.where(
        place < FIRST,
        GATHERED + y_place * FIRST + place,
        GATHERED + WORK_Y * FIRST + y_place * SECOND + place - FIRST,
    )
    places = jnp.where(at < KEPT, gathered, place)
    return places.reshape(-1, PBLK), lists, jnp.sum(beyond, axis=0)


def block_table(cited, passage_slot, passage_length, places):
    slots = pick(cited, passage_slot)
    hit = slots[..., None] == jnp.arange(passage_length.shape[0])
    blocks = jnp.sum(jnp.where(hit, passage_length, 0), axis=-1)
    found = jnp.sum(jnp.where(hit[..., None], places, 0), axis=2)
    earlier = jnp.arange(CITED_PASSAGES)
    earlier = earlier[:, None] < earlier[None, :]
    begins = jnp.sum(jnp.where(earlier, blocks[:, :, None], 0), axis=1)
    block = jnp.arange(PBLK)
    order = jnp.where(block < blocks[..., None], begins[..., None] + block, -1)
    mine = order[..., None] == jnp.arange(MOST + 1)
    table = jnp.sum(jnp.where(mine, found[..., None], 0), axis=(1, 2))
    return table.reshape(-1), jnp.sum(blocks, axis=1)


def body(
    passage_query,
    passage_key_value,
    passage_length,
    passage_slot,
    cites,
    question_query,
    question_key_value,
    question_length,
):
    worker = lax.axis_index("work")
    z, y = worker // WORK_Y, worker % WORK_Y
    kept, *beyond = order(passage_length, passage_key_value)
    pieces = [lax.all_gather(kept, "work", axis=0, tiled=True)]
    places, lists, live = block_places(passage_length, y)

    facts = jnp.concatenate([cites, question_length[:, None]], axis=1).astype(jnp.bfloat16)
    facts = jnp.pad(facts, ((0, 15), (0, HEAD_SIZE - CITED_PASSAGES - 1)))
    payload = bundle(question_query, question_key_value.reshape(QUESTION_LENGTH, -1), facts)
    payload = lax.all_to_all(payload, "req", 0, 0, tiled=True)

    if EXTRA:
        beyond = ring_z(beyond[0])
        z_from = (z - jnp.asarray([Z_ORDER.index(i) for i in range(WORK_Z)])) % WORK_Z
        mine = jnp.sum(jnp.where(jnp.arange(WORK_Y)[:, None] == y, lists, 0), axis=1)
        hit = z_from[:, None] == jnp.arange(WORK_Z)
        mine = jnp.sum(jnp.where(hit[..., None], mine[None], 0), axis=1)
        first, second = pack(mine.reshape(-1), beyond)
        pieces.append(jnp.concatenate(ring_y(first), axis=0))
        pieces.append(
            lax.cond(
                jnp.max(live) > FIRST,
                lambda part: jnp.concatenate(ring_y(part), axis=0),
                lambda part: jnp.zeros((WORK_Y * SECOND, *part.shape[1:]), part.dtype),
                second,
            )
        )

    slot_total = passage_query.shape[0] // PASSAGE_ROWS
    my_blocks = lax.dynamic_slice_in_dim(passage_length, worker * slot_total, slot_total)
    passage_output = passage_attention(my_blocks, passage_query, passage_key_value)

    facts = payload[:, FACT_ROW, : CITED_PASSAGES + 1].astype(jnp.int32)
    table, count = block_table(facts[:, :CITED_PASSAGES], passage_slot, passage_length, places)
    answer = question_attention(table, count, facts[:, CITED_PASSAGES], payload, pieces)
    answer = lax.all_to_all(answer, "req", 0, 0, tiled=True)
    return passage_output, spread(answer)


def solution(mesh):
    return jax.shard_map(
        body,
        mesh=mesh,
        in_specs=(
            P("work", "req"),
            P(None, "work", "req"),
            P(),
            P(),
            P(("req", "work"), None),
            P(("req", "work"), None),
            P(("req", "work"), None, None),
            P(("req", "work")),
        ),
        out_specs=(P("work", "req"), P(("req", "work"), None)),
        check_vma=False,
    )
```

```python
import math

import jax
import jax.numpy as jnp
from jax import lax
from jax.experimental import pallas as pl
from jax.experimental.pallas import tpu as pltpu
from jax.sharding import PartitionSpec as P

QUERY_HEADS = 64
KEY_VALUE_HEADS = 8
GROUP = QUERY_HEADS // KEY_VALUE_HEADS
HEAD_SIZE = 128
BLOCK = 128
PBLK = 4
CITED_PASSAGES = 4
QUESTION_LENGTH = 128
PASSAGE_ROWS = 512
SCALE = math.log2(math.e) / math.sqrt(HEAD_SIZE)
LOW = -1e30
TILE = 64
LOTS = 2
MOST = CITED_PASSAGES * PBLK
WORK_Z, WORK_Y = 8, 4
SLOTS = 2
KEPT = 6
EXTRA = SLOTS * PBLK - KEPT
FIRST = 6
SECOND = WORK_Z * EXTRA - FIRST
GATHERED = WORK_Z * WORK_Y * KEPT
Z_ORDER = (0, 1, 3, 5, 7, 6, 4, 2)
Y_ORDER = (0, 1, 3, 2)
OWN_ROW = GROUP * QUESTION_LENGTH
FACT_ROW = OWN_ROW + 2 * QUESTION_LENGTH
PAYLOAD = FACT_ROW + 16
DOT_NT = (((1,), (1,)), ((), ()))


def stack_heads(ref_rows):
    return jnp.concatenate(
        [ref_rows[:, h * HEAD_SIZE : (h + 1) * HEAD_SIZE] for h in range(GROUP)], axis=0
    )


def with_ones(values):
    return jnp.concatenate([values, jnp.ones_like(values)], axis=1)


def passage_kernel(blocks_ref, q_ref, kv_ref, out_ref):
    slot = pl.program_id(0)
    blocks = blocks_ref[slot]
    rows = GROUP * BLOCK
    row = lax.broadcasted_iota(jnp.int32, (rows, BLOCK), 0) % BLOCK
    column = lax.broadcasted_iota(jnp.int32, (rows, BLOCK), 1)
    causal = column <= row
    for i in range(PBLK):
        place = slice(i * BLOCK, (i + 1) * BLOCK)

        @pl.when(i < blocks)
        def _():
            q = stack_heads(q_ref[place, :])
            k = kv_ref[0, : (i + 1) * BLOCK, :]
            v = with_ones(kv_ref[1, : (i + 1) * BLOCK, :])
            s = lax.dot_general(q, k, DOT_NT, preferred_element_type=jnp.float32)
            last = jnp.where(causal, s[:, i * BLOCK :], LOW)
            s = last if i == 0 else jnp.concatenate([s[:, : i * BLOCK], last], axis=1)
            m = jnp.max(s, axis=1, keepdims=True)
            p = jnp.exp2((s - m) * SCALE).astype(jnp.bfloat16)
            o = jnp.dot(p, v, preferred_element_type=jnp.float32)
            o = (o[:, :HEAD_SIZE] / o[:, HEAD_SIZE:]).astype(jnp.bfloat16)
            for h in range(GROUP):
                out_ref[place, h * HEAD_SIZE : (h + 1) * HEAD_SIZE] = o[h * BLOCK : (h + 1) * BLOCK]

        @pl.when(i >= blocks)
        def _():
            out_ref[place, :] = jnp.zeros((BLOCK, GROUP * HEAD_SIZE), jnp.bfloat16)


def passage_attention(blocks, query, key_value):
    slots = query.shape[0] // PASSAGE_ROWS
    width = GROUP * HEAD_SIZE
    return pl.pallas_call(
        passage_kernel,
        out_shape=jax.ShapeDtypeStruct(query.shape, jnp.bfloat16),
        grid_spec=pltpu.PrefetchScalarGridSpec(
            num_scalar_prefetch=1,
            grid=(slots,),
            in_specs=[
                pl.BlockSpec((PASSAGE_ROWS, width), lambda s, b: (s, 0)),
                pl.BlockSpec((2, PASSAGE_ROWS, HEAD_SIZE), lambda s, b: (0, s, 0)),
            ],
            out_specs=pl.BlockSpec((PASSAGE_ROWS, width), lambda s, b: (s, 0)),
        ),
        compiler_params=pltpu.CompilerParams(vmem_limit_bytes=40 * 1024 * 1024),
        cost_estimate=pl.CostEstimate(
            flops=slots * 4 * 1024 * 512 * 512, bytes_accessed=5 * 1024 * 1024, transcendentals=0
        ),
    )(blocks, query, key_value)


def bundle_kernel(q_ref, k_ref, v_ref, facts_ref, out_ref):
    for h in range(GROUP):
        out_ref[0, h * QUESTION_LENGTH : (h + 1) * QUESTION_LENGTH, :] = q_ref[
            :, h * HEAD_SIZE : (h + 1) * HEAD_SIZE
        ]
    out_ref[0, OWN_ROW : OWN_ROW + QUESTION_LENGTH, :] = k_ref[...].T
    out_ref[0, OWN_ROW + QUESTION_LENGTH : FACT_ROW, :] = v_ref[...]
    out_ref[0, FACT_ROW:, :] = facts_ref[...]


def bundle(query, own, facts):
    width = GROUP * HEAD_SIZE
    return pl.pallas_call(
        bundle_kernel,
        out_shape=jax.ShapeDtypeStruct((KEY_VALUE_HEADS, PAYLOAD, HEAD_SIZE), jnp.bfloat16),
        grid=(KEY_VALUE_HEADS,),
        in_specs=[
            pl.BlockSpec((QUESTION_LENGTH, width), lambda g: (0, g)),
            pl.BlockSpec((QUESTION_LENGTH, HEAD_SIZE), lambda g: (0, g)),
            pl.BlockSpec((QUESTION_LENGTH, HEAD_SIZE), lambda g: (0, KEY_VALUE_HEADS + g)),
            pl.BlockSpec((16, HEAD_SIZE), lambda g: (0, 0)),
        ],
        out_specs=pl.BlockSpec((1, PAYLOAD, HEAD_SIZE), lambda g: (g, 0, 0)),
        cost_estimate=pl.CostEstimate(flops=0, bytes_accessed=5 * 1024 * 1024, transcendentals=0),
    )(query, own, own, facts)


def spread_kernel(in_ref, out_ref):
    for g in range(in_ref.shape[0]):
        for h in range(GROUP):
            first = (g * GROUP + h) * HEAD_SIZE
            out_ref[:, first : first + HEAD_SIZE] = in_ref[
                g, h * QUESTION_LENGTH : (h + 1) * QUESTION_LENGTH, :
            ]


def spread(answer):
    groups = 4
    width = groups * GROUP * HEAD_SIZE
    return pl.pallas_call(
        spread_kernel,
        out_shape=jax.ShapeDtypeStruct((QUESTION_LENGTH, QUERY_HEADS * HEAD_SIZE), jnp.bfloat16),
        grid=(KEY_VALUE_HEADS // groups,),
        in_specs=[pl.BlockSpec((groups, OWN_ROW, HEAD_SIZE), lambda g: (g, 0, 0))],
        out_specs=pl.BlockSpec((QUESTION_LENGTH, width), lambda g: (0, g)),
        cost_estimate=pl.CostEstimate(flops=0, bytes_accessed=4 * 1024 * 1024, transcendentals=0),
    )(answer)


def order_kernel(length_ref, kv_ref, kept_ref, *refs):
    worker = lax.axis_index("work")
    before = 0
    for slot in range(SLOTS):
        length = length_ref[worker * SLOTS + slot]
        for block in range(PBLK):
            rows = slice((slot * PBLK + block) * BLOCK, (slot * PBLK + block + 1) * BLOCK)

            def put(ref, place):
                ref[place, 0] = kv_ref[0, rows, :].T
                ref[place, 1] = kv_ref[1, rows, :]

            place = before + block
            pl.when((block < length) & (place < KEPT))(lambda place=place: put(kept_ref, place))
            if refs:
                pl.when((block < length) & (place >= KEPT))(
                    lambda place=place: put(refs[0], place - KEPT)
                )
        before = before + length


def order(passage_length, key_value):
    shapes = [
        jax.ShapeDtypeStruct((size, 2, BLOCK, HEAD_SIZE), jnp.bfloat16)
        for size in (KEPT, EXTRA)
        if size
    ]
    return pl.pallas_call(
        order_kernel,
        out_shape=shapes,
        in_specs=[pl.BlockSpec(memory_space=pltpu.SMEM), pl.BlockSpec(memory_space=pltpu.VMEM)],
        out_specs=[pl.BlockSpec(memory_space=pltpu.VMEM)] * len(shapes),
        cost_estimate=pl.CostEstimate(flops=0, bytes_accessed=1024 * 1024, transcendentals=0),
    )(passage_length, key_value)


def pack_kernel(place_ref, *refs):
    sources, outs = refs[:-2], refs[-2:]
    blocks = [(source, i) for source in sources for i in range(source.shape[0])]
    for index, (source, i) in enumerate(blocks):
        place = place_ref[index]

        @pl.when((place >= 0) & (place < FIRST))
        def _():
            outs[0][place] = source[i]

        @pl.when(place >= FIRST)
        def _():
            outs[1][place - FIRST] = source[i]


def pack(place, sources):
    return pl.pallas_call(
        pack_kernel,
        out_shape=[
            jax.ShapeDtypeStruct((size, *sources[0].shape[1:]), jnp.bfloat16)
            for size in (FIRST, SECOND)
        ],
        in_specs=[pl.BlockSpec(memory_space=pltpu.SMEM)]
        + [pl.BlockSpec(memory_space=pltpu.VMEM)] * len(sources),
        out_specs=[pl.BlockSpec(memory_space=pltpu.VMEM)] * 2,
        cost_estimate=pl.CostEstimate(flops=0, bytes_accessed=2 * 1024 * 1024, transcendentals=0),
    )(place, *sources)


def question_kernel(table_ref, count_ref, length_ref, in_ref, *refs):
    pieces, out_ref, store, sems = refs[:-3], refs[-3], refs[-2], refs[-1]
    request = pl.program_id(0)
    total = pl.num_programs(0)

    def start(which, carry):
        def one(index, carry):
            place = table_ref[which * (MOST + 1) + index]
            low = 0
            for piece in pieces:
                size = piece.shape[0]

                @pl.when((place >= low) & (place < low + size))
                def _():
                    pltpu.make_async_copy(
                        piece.at[place - low], store.at[which, index], sems.at[which, index]
                    ).start()

                low += size
            return carry

        return lax.fori_loop(0, count_ref[which], one, carry)

    @pl.when(request == 0)
    def _():
        lax.fori_loop(0, total, start, 0)

    length = length_ref[request]
    count = count_ref[request]

    def wait(index, carry):
        pltpu.make_async_copy(
            pieces[0].at[0], store.at[request, index], sems.at[request, index]
        ).wait()
        return carry

    lax.fori_loop(0, count, wait, 0)
    rows = GROUP // LOTS * TILE
    row = lax.broadcasted_iota(jnp.int32, (rows, BLOCK), 0) % TILE
    column = lax.broadcasted_iota(jnp.int32, (rows, BLOCK), 1)

    def attend(cited):
        @pl.when(count < cited)
        def _():
            store[request, cited - 1] = jnp.zeros(store.shape[2:], store.dtype)

        extra = jnp.where(count < cited, LOW, 0.0)

        def tile_step(tile, carry):
            first = pl.multiple_of(tile * TILE, TILE)
            k = [in_ref[0, OWN_ROW : OWN_ROW + BLOCK, :]] + [store[request, i, 0] for i in range(cited)]
            v = [in_ref[0, OWN_ROW + BLOCK : FACT_ROW, :]] + [store[request, i, 1] for i in range(cited)]
            k = jnp.concatenate(k, axis=1)
            v = with_ones(jnp.concatenate(v, axis=0))
            lot = GROUP // LOTS

            def score(heads):
                q = jnp.concatenate(
                    [in_ref[0, pl.ds(h * QUESTION_LENGTH + first, TILE), :] for h in heads], axis=0
                )
                s = jnp.dot(q, k, preferred_element_type=jnp.float32)
                return jnp.concatenate(
                    [
                        jnp.where(column <= row + first, s[:, :BLOCK], LOW),
                        s[:, BLOCK:-BLOCK],
                        s[:, -BLOCK:] + extra,
                    ],
                    axis=1,
                )

            def finish(heads, s):
                m = jnp.max(s, axis=1, keepdims=True)
                p = jnp.exp2((s - m) * SCALE).astype(jnp.bfloat16)
                o = jnp.dot(p, v, preferred_element_type=jnp.float32)
                o = o[:, :HEAD_SIZE] / o[:, HEAD_SIZE:]
                o = jnp.where(row + first < length, o, 0.0).astype(jnp.bfloat16)
                for i, h in enumerate(heads):
                    out_ref[0, pl.ds(h * QUESTION_LENGTH + first, TILE), :] = o[
                        i * TILE : (i + 1) * TILE
                    ]

            lots = [range(i * lot, (i + 1) * lot) for i in range(LOTS)]
            s = score(lots[0])
            for i in range(LOTS):
                following = score(lots[i + 1]) if i + 1 < LOTS else None
                finish(lots[i], s)
                s = following
            return carry

        lax.fori_loop(0, (length + TILE - 1) // TILE, tile_step, 0)

    def clear(tile, carry):
        for h in range(GROUP):
            out_ref[0, pl.ds(h * QUESTION_LENGTH + pl.multiple_of(tile * TILE, TILE), TILE), :] = (
                jnp.zeros((TILE, HEAD_SIZE), out_ref.dtype)
            )
        return carry

    lax.fori_loop((length + TILE - 1) // TILE, QUESTION_LENGTH // TILE, clear, 0)

    for cited in range(CITED_PASSAGES + 1, MOST + 2, 2):
        pl.when(count // 2 * 2 + 1 == cited)(lambda cited=cited: attend(cited))


def question_attention(table, count, length, payload, pieces):
    requests = payload.shape[0]
    return pl.pallas_call(
        question_kernel,
        out_shape=pltpu.HBM((requests, OWN_ROW, HEAD_SIZE), jnp.bfloat16),
        grid_spec=pltpu.PrefetchScalarGridSpec(
            num_scalar_prefetch=3,
            grid=(requests,),
            in_specs=[pl.BlockSpec((1, PAYLOAD, HEAD_SIZE), lambda r, *_: (r, 0, 0))]
            + [pl.BlockSpec(memory_space=pltpu.HBM)] * len(pieces),
            out_specs=pl.BlockSpec((1, OWN_ROW, HEAD_SIZE), lambda r, *_: (r, 0, 0)),
            scratch_shapes=[
                pltpu.VMEM((requests, MOST + 1, *pieces[0].shape[1:]), jnp.bfloat16),
                pltpu.SemaphoreType.DMA((requests, MOST)),
            ],
        ),
        compiler_params=pltpu.CompilerParams(vmem_limit_bytes=40 * 1024 * 1024),
        cost_estimate=pl.CostEstimate(
            flops=4 * 1024 * 1024 * 1024, bytes_accessed=24 * 1024 * 1024, transcendentals=0
        ),
    )(table, count, length, payload, *pieces)


def step_z(array, by):
    steps = [
        (z * WORK_Y + y, (z + by) % WORK_Z * WORK_Y + y) for z in range(WORK_Z) for y in range(WORK_Y)
    ]
    return lax.ppermute(array, "work", steps)


def step_y(array, by):
    steps = [
        (z * WORK_Y + y, z * WORK_Y + (y + by) % WORK_Y) for z in range(WORK_Z) for y in range(WORK_Y)
    ]
    return lax.ppermute(array, "work", steps)


def ring_z(chunk):
    out = [chunk]
    up = down = chunk
    for _ in range(WORK_Z // 2 - 1):
        up, down = step_z(up, 1), step_z(down, -1)
        out += [up, down]
    half = chunk.shape[0] // 2
    return out + [step_z(up[:half], 1), step_z(down[half:], -1)]


def ring_y(chunk):
    half = chunk.shape[0] // 2
    up, down = step_y(chunk, 1), step_y(chunk, -1)
    return [chunk, up, down, step_y(up[:half], 1), step_y(down[half:], -1)]


def pick(index, values):
    values = jnp.asarray(values, jnp.int32)
    return jnp.sum(
        jnp.where(index[..., None] == jnp.arange(values.shape[0]), values, 0), axis=-1
    )


def block_places(passage_length, y):
    lengths = passage_length.reshape(WORK_Z, WORK_Y, SLOTS)
    ahead = jnp.concatenate([jnp.zeros_like(lengths[..., :1]), lengths[..., :1]], axis=-1)
    at = ahead[..., None] + jnp.arange(PBLK)
    worker = jnp.arange(WORK_Z)[:, None] * WORK_Y + jnp.arange(WORK_Y)
    gathered = worker[..., None, None] * KEPT + at
    if not EXTRA:
        return gathered.reshape(-1, PBLK), None, None
    beyond = jnp.maximum(jnp.sum(lengths, axis=-1) - KEPT, 0)
    earlier = jnp.arange(WORK_Z)
    earlier = (earlier[:, None] < earlier[None, :]).astype(jnp.int32)
    begins = jnp.sum(earlier[:, :, None] * beyond[:, None, :], axis=0)
    index = jnp.arange(EXTRA)
    lists = jnp.where(index < beyond[..., None], begins[..., None] + index, -1)
    place = begins[..., None, None] + at - KEPT
    y_place = pick((y - jnp.arange(WORK_Y)) % WORK_Y, Y_ORDER)[None, :, None, None]
    place = jnp.where(
        place < FIRST,
        GATHERED + y_place * FIRST + place,
        GATHERED + WORK_Y * FIRST + y_place * SECOND + place - FIRST,
    )
    places = jnp.where(at < KEPT, gathered, place)
    return places.reshape(-1, PBLK), lists, jnp.sum(beyond, axis=0)


def block_table(cited, passage_slot, passage_length, places):
    slots = pick(cited, passage_slot)
    hit = slots[..., None] == jnp.arange(passage_length.shape[0])
    blocks = jnp.sum(jnp.where(hit, passage_length, 0), axis=-1)
    found = jnp.sum(jnp.where(hit[..., None], places, 0), axis=2)
    earlier = jnp.arange(CITED_PASSAGES)
    earlier = earlier[:, None] < earlier[None, :]
    begins = jnp.sum(jnp.where(earlier, blocks[:, :, None], 0), axis=1)
    block = jnp.arange(PBLK)
    order = jnp.where(block < blocks[..., None], begins[..., None] + block, -1)
    mine = order[..., None] == jnp.arange(MOST + 1)
    table = jnp.sum(jnp.where(mine, found[..., None], 0), axis=(1, 2))
    return table.reshape(-1), jnp.sum(blocks, axis=1)


def body(
    passage_query,
    passage_key_value,
    passage_length,
    passage_slot,
    cites,
    question_query,
    question_key_value,
    question_length,
):
    worker = lax.axis_index("work")
    z, y = worker // WORK_Y, worker % WORK_Y
    kept, *beyond = order(passage_length, passage_key_value)
    pieces = [lax.all_gather(kept, "work", axis=0, tiled=True)]
    places, lists, live = block_places(passage_length, y)

    facts = jnp.concatenate([cites, question_length[:, None]], axis=1).astype(jnp.bfloat16)
    facts = jnp.pad(facts, ((0, 15), (0, HEAD_SIZE - CITED_PASSAGES - 1)))
    payload = bundle(question_query, question_key_value.reshape(QUESTION_LENGTH, -1), facts)
    payload = lax.all_to_all(payload, "req", 0, 0, tiled=True)

    if EXTRA:
        beyond = ring_z(beyond[0])
        z_from = (z - jnp.asarray([Z_ORDER.index(i) for i in range(WORK_Z)])) % WORK_Z
        mine = jnp.sum(jnp.where(jnp.arange(WORK_Y)[:, None] == y, lists, 0), axis=1)
        hit = z_from[:, None] == jnp.arange(WORK_Z)
        mine = jnp.sum(jnp.where(hit[..., None], mine[None], 0), axis=1)
        first, second = pack(mine.reshape(-1), beyond)
        pieces.append(jnp.concatenate(ring_y(first), axis=0))
        pieces.append(
            lax.cond(
                jnp.max(live) > FIRST,
                lambda part: jnp.concatenate(ring_y(part), axis=0),
                lambda part: jnp.zeros((WORK_Y * SECOND, *part.shape[1:]), part.dtype),
                second,
            )
        )

    slot_total = passage_query.shape[0] // PASSAGE_ROWS
    my_blocks = lax.dynamic_slice_in_dim(passage_length, worker * slot_total, slot_total)
    passage_output = passage_attention(my_blocks, passage_query, passage_key_value)

    facts = payload[:, FACT_ROW, : CITED_PASSAGES + 1].astype(jnp.int32)
    table, count = block_table(facts[:, :CITED_PASSAGES], passage_slot, passage_length, places)
    answer = question_attention(table, count, facts[:, CITED_PASSAGES], payload, pieces)
    answer = lax.all_to_all(answer, "req", 0, 0, tiled=True)
    return passage_output, spread(answer)


def solution(mesh):
    return jax.shard_map(
        body,
        mesh=mesh,
        in_specs=(
            P("work", "req"),
            P(None, "work", "req"),
            P(),
            P(),
            P(("req", "work"), None),
            P(("req", "work"), None),
            P(("req", "work"), None, None),
            P(("req", "work")),
        ),
        out_specs=(P("work", "req"), P(("req", "work"), None)),
        check_vma=False,
    )
```
